512 devices in a mesh: worker: 16 (over z), fsdp: 16 (over y_lo, x, core), tensor: 2 (over y_hi).
Axes of the slice: x: 4, y: 4 (y_hi: 2, y_lo: 2; y = y_hi * 2 + y_lo), z: 16, core: 2. Of those that a mesh axis runs over, the one named last changes fastest.
Arguments:
- token_ids: int32 [16, 4096], P('worker', 'fsdp'), may hold values from 0 to 128255, as said below
- features_in: bfloat16 [16, 4096, 8192], P('worker', 'fsdp', 'tensor')
- targets: bfloat16 [16, 4096, 512], P('worker', 'fsdp', 'tensor'), may hold values from -6 to 6
- local_weight: bfloat16 [16, 8192, 512], P('worker', 'fsdp', 'tensor'), may hold values from -0.0625 to 0.0625
- adam_first: bfloat16 [16, 8192, 512], P('worker', 'fsdp', 'tensor'), may hold values from -0.00390625 to 0.00390625
- adam_second: bfloat16 [16, 8192, 512], P('worker', 'fsdp', 'tensor'), may hold values from 9.95351e-09 to 9.983778e-07
- prev_delta: bfloat16 [16, 8192, 512], P('worker', 'fsdp', 'tensor'), may hold values from -0.046875 to 0.046875
- global_weight: bfloat16 [8192, 512], P('fsdp', 'tensor'), may hold values from -0.0625 to 0.0625
- outer_momentum: bfloat16 [8192, 512], P('fsdp', 'tensor'), may hold values from -0.046875 to 0.046875
- fragment_of_tile: int32 [64, 4], P('fsdp'), may hold values from 0 to 1, as said below
Outputs:
- new_local: bfloat16 [16, 8192, 512], P('worker', 'fsdp', 'tensor')
- new_first: bfloat16 [16, 8192, 512], P('worker', 'fsdp', 'tensor')
- new_second: bfloat16 [16, 8192, 512], P('worker', 'fsdp', 'tensor')
- new_global: bfloat16 [8192, 512], P('fsdp', 'tensor')
- new_momentum: bfloat16 [8192, 512], P('fsdp', 'tensor')
The draws below stay inside these ranges and needn't reach their ends.
Inputs may be any that keep to these rules, and one draw needn't show every extreme that they name: `token_ids`: 0 marks padding; in each replica's row the first 1024 tokens or more are not padding, and padding only follows the last non-padding token. `fragment_of_tile`: every row of tiles holds 2 tiles of each of the 2 rounds.
All inputs are finite; a program needn't handle non-finite values.
Results may differ from the reference program's by a relative error of at most 0.02.
Values may be sent and summed in bfloat16 or wider, within the bound.
No kernel may reach another device: no remote copies, remote signals or barrier semaphores. Data moves between devices by JAX's collectives and lax.ppermute only.
A program may use at most 64 MiB of HBM per device.

```python
import math
import jax
import jax.numpy as jnp
from jax import lax

D = 8192
HD = 128
KVH = 4
VOCAB = 128256
FRAGS = 2
TOK_DEV = 256
KW = 512
TOKENS = 4096
N_WORKER = 16
N_FSDP = 16


def draw_token_ids(key, part):
    key = jax.random.fold_in(key, 11)
    key_ids, key_len = jax.random.split(key)
    ids = jax.random.randint(key_ids, (N_WORKER, TOKENS), 1, VOCAB)
    lengths = jax.random.randint(key_len, (N_WORKER, 1), TOKENS // 4, TOKENS + 1)
    position = jnp.arange(TOKENS)[None, :]
    return jnp.where(position < lengths, ids, 0).astype(jnp.int32)


def draw_features_in(key, part):
    key = jax.random.fold_in(key, 37)
    ramp = jnp.arange(D, dtype=jnp.float32) / (D - 1)
    base = jnp.clip(jax.random.normal(key, (N_WORKER, TOKENS, D), jnp.float32), -6.0, 6.0)
    scale = jnp.exp(ramp * jnp.log(4.0))
    return (base * scale[None, None, :]).astype(jnp.bfloat16)


def draw_fragment_of_tile(key, part):
    key = jax.random.fold_in(key, 23)
    keys = jax.random.split(key, D // HD)
    orders = jax.vmap(lambda k: jax.random.permutation(k, KVH))(keys)
    return (orders % FRAGS).astype(jnp.int32)


def block_levels(stream_key, shape, cuts, low, high):
    gain, own = 1.0, jax.random.fold_in(stream_key, 6)
    for axis_at, parts in cuts:
        draws = jnp.exp(jax.random.uniform(jax.random.fold_in(own, axis_at), (parts,), jnp.float32, low / len(cuts), high / len(cuts)))
        gain = gain * jnp.repeat(draws, shape[axis_at] // parts).reshape([-1 if axis == axis_at else 1 for axis in range(len(shape))])
    return gain


def normal_values(key, extent, width, most, pieces=(), kind=jnp.bfloat16):
    array = width * jax.random.normal(key, extent, jnp.float32)
    if pieces:
        array = array * block_levels(key, extent, pieces, -0.22, 0.18)
    return jnp.clip(array, -most, most).astype(kind)


def setup_inputs(seed: int = 0) -> dict:
    arg_keys = jax.random.split(jax.random.key(seed), 11)
    return {
        "token_ids": draw_token_ids(jax.random.fold_in(arg_keys[10], 71), 0),
        "features_in": draw_features_in(jax.random.fold_in(arg_keys[10], 71), 0),
        "targets": normal_values(arg_keys[2], (N_WORKER, TOKENS, KW), 1.0, 6.0, ((0, 16), (1, 16), (2, 2))),
        "local_weight": normal_values(arg_keys[3], (N_WORKER, D, KW), D ** -0.5, 0.0625, ((0, 16), (1, 16), (2, 2))),
        "adam_first": normal_values(arg_keys[4], (N_WORKER, D, KW), 0.0003, 0.00390625, ((0, 16), (1, 16), (2, 2))),
        "adam_second": jnp.clip(jnp.exp(math.log(9.98377799987793e-07) - 4.6082065 * jax.random.uniform(arg_keys[5], (N_WORKER, D, KW), jnp.float32) ** block_levels(arg_keys[5], (N_WORKER, D, KW), ((0, 16), (1, 16), (2, 2)), -0.2, 0.2)), 9.953510016202927e-09, 9.98377799987793e-07).astype(jnp.bfloat16),
        "prev_delta": normal_values(arg_keys[6], (N_WORKER, D, KW), 0.003, 0.046875, ((0, 16), (1, 16), (2, 2))),
        "global_weight": normal_values(arg_keys[7], (D, KW), D ** -0.5, 0.0625, ((0, 16), (1, 2))),
        "outer_momentum": normal_values(arg_keys[8], (D, KW), 0.003, 0.046875, ((0, 16), (1, 2))),
        "fragment_of_tile": draw_fragment_of_tile(jax.random.fold_in(arg_keys[10], 71), 0),
    }


def inner_step(pack):
    ids, feats, target, weight, first_in, second_in = pack
    values = feats.astype(jnp.float32)
    inv = lax.rsqrt(lax.optimization_barrier(jnp.mean(values * values, axis=1, keepdims=True)) + 1e-05)
    normed = (values * inv).astype(jnp.bfloat16)
    mask = (ids != 0).astype(jnp.float32)
    keys = jnp.dot(normed, weight, preferred_element_type=jnp.float32)
    resid = ((keys - target.astype(jnp.float32)) * mask[:, None]).astype(jnp.bfloat16)
    blocks_x = normed.reshape(N_FSDP, TOK_DEV, D)
    blocks_r = resid.reshape(N_FSDP, TOK_DEV, KW)

    def accumulate(total, pair):
        left, right = pair
        term = lax.dot_general(left, right, (((0,), (0,)), ((), ())), preferred_element_type=jnp.float32)
        rounded = lax.optimization_barrier(term.astype(jnp.bfloat16))
        return (total + rounded.astype(jnp.float32), None)
    raw, _ = lax.scan(accumulate, jnp.zeros((D, KW), jnp.float32), (blocks_x, blocks_r))
    norm = jnp.sqrt(jnp.sum(raw * raw))
    clipped = raw * jnp.minimum(1.0, 1.0 / (norm + 1e-06))
    first = 0.9 * first_in.astype(jnp.float32) + 0.1 * clipped
    second = 0.95 * second_in.astype(jnp.float32) + 0.05 * clipped * clipped
    old = weight.astype(jnp.float32)
    stepped = old - 0.0004 * (first / (jnp.sqrt(second) + 1e-08) + 0.1 * old)
    return (stepped, first.astype(jnp.bfloat16), second.astype(jnp.bfloat16))

def reference(token_ids, features_in, targets, local_weight, adam_first, adam_second, prev_delta, global_weight, outer_momentum, fragment_of_tile):
    stepped, new_first, new_second = lax.map(inner_step, (token_ids, features_in, targets, local_weight, adam_first, adam_second))
    outer_grad = lax.optimization_barrier(jnp.sum(prev_delta.astype(jnp.float32), axis=0)) / N_WORKER
    momentum = 0.9 * outer_momentum.astype(jnp.float32) + outer_grad
    merged = global_weight.astype(jnp.float32) - 0.7 * (outer_grad + 0.9 * momentum)
    selected = jnp.repeat(jnp.repeat(fragment_of_tile == 0, HD, axis=0), HD, axis=1)
    new_momentum = jnp.where(selected, momentum.astype(jnp.bfloat16), outer_momentum)
    new_global = jnp.where(selected, merged.astype(jnp.bfloat16), global_weight)
    mixed = 0.5 * stepped + 0.5 * new_global.astype(jnp.float32)[None]
    new_local = jnp.where(selected[None], mixed, stepped).astype(jnp.bfloat16)
    return (new_local, new_first, new_second, new_global, new_momentum)
```

```python
import jax
import jax.numpy as jnp
from jax import lax
from jax.sharding import Mesh, PartitionSpec as P

HD = 128
WORKER = ("zh", "zl")
FSDP = ("ylo", "x", "core")
GROUP = ("x", "ylo")
PLANE = ("ylo", "x", "core", "tensor")
SIZES = {"ylo": 2, "x": 4, "core": 2, "tensor": 2}
BF = jnp.bfloat16
F32 = jnp.float32


def permute(value, axes, move):
    places = [()]
    for axis in axes:
        places = [p + (i,) for p in places for i in range(SIZES[axis])]
    number = {p: n for n, p in enumerate(places)}
    pairs = [(n, number[move(*p)]) for p, n in number.items()]
    return lax.ppermute(value, axes if len(axes) > 1 else axes[0], pairs)


def swap(value, axis):
    return permute(value, (axis,), lambda i: (1 - i,))


def local(
    token_ids,
    features_in,
    targets,
    local_weight,
    adam_first,
    adam_second,
    prev_delta,
    global_weight,
    outer_momentum,
    fragment_of_tile,
):
    weight = local_weight[0]
    rows, cols = weight.shape
    core = lax.axis_index("core")
    side = lax.axis_index("tensor")
    replicas = lax.axis_size("zh") * lax.axis_size("zl")
    group = lax.axis_size("x") * lax.axis_size("ylo")

    with jax.named_scope("outer_sum"):
        delta_sum = lax.psum(prev_delta[0], "zl")
        delta_sum = lax.psum(delta_sum, "zh").astype(F32)

    with jax.named_scope("weight_move"):
        moved = permute(weight, PLANE, lambda yl, x, c, t: (c, x, t, yl))

    with jax.named_scope("own_tokens"):
        mine = features_in[0]
        tokens, half = mine.shape
        squares = jnp.sum(jnp.square(mine.astype(F32)), axis=1)
        mask = (token_ids[0] != 0).astype(F32)
    with jax.named_scope("core_swap"):
        other = swap(mine, "core")
        note = jnp.concatenate(
            [targets[0].astype(F32), squares[None], mask[None]], axis=0
        )
        note_other = swap(note, "core")
    both = jnp.concatenate([mine, other], axis=0)
    target2 = jnp.concatenate([note[:tokens], note_other[:tokens]], axis=0)
    squares2 = jnp.concatenate([note[tokens], note_other[tokens]])
    mask2 = jnp.concatenate([note[tokens + 1], note_other[tokens + 1]])
    with jax.named_scope("squares_swap"):
        squares2 = squares2 + swap(squares2, "tensor")
    inv = lax.rsqrt(squares2 / (2 * half) + 1e-05)

    with jax.named_scope("weight_gather"):
        copies = jnp.broadcast_to(moved[None], (group, rows, cols))
        matrix = lax.all_to_all(copies, GROUP, 0, 0).reshape(group * rows, cols)

    with jax.named_scope("keys"):
        part = jnp.dot(both, matrix, preferred_element_type=F32) * inv[:, None]
        part = jnp.where(core == side, part - target2, part)
        theirs = swap(part.astype(BF), "tensor")
        scale = (inv * mask2)[:, None]
        resid = ((part + theirs.astype(F32)) * scale).astype(BF)

    with jax.named_scope("gradient"):
        term = lax.dot_general(
            both, resid, (((0,), (0,)), ((), ())), preferred_element_type=F32
        ).astype(BF)
        terms = lax.all_to_all(term.reshape(group, rows, cols), GROUP, 0, 0)
        total = jnp.sum(terms.astype(F32), axis=0)
    with jax.named_scope("gradient_home"):
        raw = permute(total.astype(BF), PLANE, lambda yl, x, c, t: (t, x, yl, c)).astype(F32)
    with jax.named_scope("norm"):
        partial = jnp.broadcast_to(jnp.sum(total * total), (32, 128))
        norm = jnp.sqrt(jnp.sum(lax.all_to_all(partial, PLANE, 0, 0)[:, 0]))

    clipped = raw * jnp.minimum(1.0, 1.0 / (norm + 1e-06))
    first = 0.9 * adam_first[0].astype(F32) + 0.1 * clipped
    second = 0.95 * adam_second[0].astype(F32) + 0.05 * clipped * clipped
    old = weight.astype(F32)
    stepped = old - 0.0004 * (first / (jnp.sqrt(second) + 1e-08) + 0.1 * old)

    outer_grad = delta_sum / replicas
    momentum = 0.9 * outer_momentum.astype(F32) + outer_grad
    merged = global_weight.astype(F32) - 0.7 * (outer_grad + 0.9 * momentum)
    heads = cols // HD
    tiles = lax.dynamic_slice_in_dim(fragment_of_tile, side * heads, heads, 1)
    selected = jnp.repeat(jnp.repeat(tiles == 0, HD, axis=0), HD, axis=1)
    new_momentum = jnp.where(selected, momentum.astype(BF), outer_momentum)
    new_global = jnp.where(selected, merged.astype(BF), global_weight)
    mixed = 0.5 * stepped + 0.5 * new_global.astype(F32)
    new_local = jnp.where(selected, mixed, stepped).astype(BF)
    return (
        new_local[None],
        first.astype(BF)[None],
        second.astype(BF)[None],
        new_global,
        new_momentum,
    )


def solution(mesh):
    fine = Mesh(
        mesh.devices.reshape(4, 4, *SIZES.values()), (*WORKER, *SIZES)
    )
    state = P(WORKER, FSDP, "tensor")
    outer = P(FSDP, "tensor")
    return jax.shard_map(
        local,
        mesh=fine,
        in_specs=(
            P(WORKER, FSDP),
            state,
            state,
            state,
            state,
            state,
            state,
            outer,
            outer,
            P(FSDP, None),
        ),
        out_specs=(state, state, state, outer, outer),
        check_vma=False,
    )
```

```python
import jax
import jax.numpy as jnp
from jax import lax
from jax.experimental import pallas as pl
from jax.experimental.pallas import tpu as pltpu
from jax.sharding import Mesh, PartitionSpec as P

HD = 128
WORKER = "worker"
FSDP = ("ylo", "x", "core")
GROUP = ("x", "ylo")
PLANE = ("ylo", "x", "core", "tensor")
SIZES = {
    "worker": 16,
    "ylo": 2,
    "x": 4,
    "core": 2,
    "tensor": 2,
}
BF = jnp.bfloat16
F32 = jnp.float32
VMEM_LIMIT = 32 * 2**20


def permute(value, axes, move):
    places = [()]
    for axis in axes:
        places = [p + (i,) for p in places for i in range(SIZES[axis])]
    number = {p: n for n, p in enumerate(places)}
    pairs = [(n, number[move(*p)]) for p, n in number.items()]
    return lax.ppermute(value, axes if len(axes) > 1 else axes[0], pairs)


def swap(value, axis):
    return permute(value, (axis,), lambda i: (1 - i,))


def after(value, *others):
    return lax.optimization_barrier((value, *others))[0]


def call(kernel, name, grid, ins, in_specs, outs, out_specs, scratch=(), flops=0):
    moved = sum(a.size * a.dtype.itemsize for a in (*ins, *outs))
    return pl.pallas_call(
        kernel,
        grid=grid,
        in_specs=in_specs,
        out_specs=out_specs,
        out_shape=outs,
        scratch_shapes=scratch,
        name=name,
        compiler_params=pltpu.CompilerParams(vmem_limit_bytes=VMEM_LIMIT),
        cost_estimate=pl.CostEstimate(
            flops=flops, bytes_accessed=moved, transcendentals=0
        ),
    )(*ins)


def sum_kernel(terms, total, squares, so_far):
    step = pl.program_id(0)
    value = jnp.sum(terms[...].astype(F32), axis=0)
    total[...] = value.astype(BF)

    @pl.when(step == 0)
    def _():
        so_far[...] = jnp.zeros_like(so_far)

    so_far[...] += jnp.sum(value * value, axis=0, keepdims=True)

    @pl.when(step == pl.num_programs(0) - 1)
    def _():
        squares[...] = jnp.full(squares.shape, jnp.sum(so_far[...]), F32)


def sum_terms(terms, places):
    group, rows, cols = terms.shape
    part = rows // 4
    return call(
        sum_kernel,
        "sum_terms",
        (rows // part,),
        (terms,),
        [pl.BlockSpec((group, part, cols), lambda k: (0, k, 0))],
        [
            jax.ShapeDtypeStruct((rows, cols), BF),
            jax.ShapeDtypeStruct((places, 128), F32),
        ],
        [
            pl.BlockSpec((part, cols), lambda k: (k, 0)),
            pl.BlockSpec((places, 128), lambda k: (0, 0)),
        ],
        [pltpu.VMEM((1, cols), F32)],
    )


def update_kernel(
    replicas,
    spot,
    fragment,
    squares,
    raw,
    adam_first,
    adam_second,
    weight,
    global_weight,
    outer_momentum,
    delta_sum,
    new_local,
    new_first,
    new_second,
    new_global,
    new_momentum,
):
    step = pl.program_id(0)
    norm = jnp.sqrt(jnp.sum(squares[...], axis=0, keepdims=True)[:, :1])
    clip = jnp.minimum(1.0, 1.0 / (norm + 1e-06))
    heads = raw.shape[1] // HD
    for head in range(heads):
        at = (slice(None), slice(head * HD, (head + 1) * HD))
        clipped = raw[at].astype(F32) * clip
        first = 0.9 * adam_first[at].astype(F32) + 0.1 * clipped
        second = 0.95 * adam_second[at].astype(F32) + 0.05 * clipped * clipped
        old = weight[at].astype(F32)
        stepped = old - 0.0004 * (first / (jnp.sqrt(second) + 1e-08) + 0.1 * old)
        new_first[at] = first.astype(BF)
        new_second[at] = second.astype(BF)
        chosen = fragment[step, spot[0] * heads + head] == 0

        @pl.when(chosen)
        def _():
            outer_grad = delta_sum[at] / replicas
            momentum = 0.9 * outer_momentum[at].astype(F32) + outer_grad
            merged = global_weight[at].astype(F32) - 0.7 * (
                outer_grad + 0.9 * momentum
            )
            merged = merged.astype(BF)
            new_momentum[at] = momentum.astype(BF)
            new_global[at] = merged
            new_local[at] = (0.5 * stepped + 0.5 * merged.astype(F32)).astype(BF)

        @pl.when(jnp.logical_not(chosen))
        def _():
            new_momentum[at] = outer_momentum[at]
            new_global[at] = global_weight[at]
            new_local[at] = stepped.astype(BF)


def update(replicas, spot, fragment, squares, arrays):
    rows, cols = arrays[0].shape
    block = pl.BlockSpec((HD, cols), lambda k: (k, 0))
    smem = pl.BlockSpec(memory_space=pltpu.SMEM)
    return call(
        lambda *refs: update_kernel(replicas, *refs),
        "update",
        (rows // HD,),
        (spot, fragment, squares, *arrays),
        [smem, smem, pl.BlockSpec(squares.shape, lambda k: (0, 0))]
        + [block] * len(arrays),
        [jax.ShapeDtypeStruct((rows, cols), BF)] * 5,
        [block] * 5,
    )


def local(
    token_ids,
    features_in,
    targets,
    local_weight,
    adam_first,
    adam_second,
    prev_delta,
    global_weight,
    outer_momentum,
    fragment_of_tile,
):
    weight = local_weight[0]
    rows, cols = weight.shape
    core = lax.axis_index("core")
    side = lax.axis_index("tensor")
    replicas = lax.axis_size(WORKER)
    group = lax.axis_size("x") * lax.axis_size("ylo")
    mine = features_in[0]
    tokens, half = mine.shape

    with jax.named_scope("weight_move"):
        moved = permute(weight, PLANE, lambda yl, x, c, t: (c, x, t, yl))

    with jax.named_scope("squares"):
        squares = jnp.sum(jnp.square(mine.astype(F32)), axis=1)
        squares = squares + swap(squares, "tensor")

    with jax.named_scope("weight_gather"):
        copies = jnp.broadcast_to(moved[None], (group, rows, cols))
        copies, squares = lax.optimization_barrier((copies, squares))
        matrix = lax.all_to_all(copies, GROUP, 0, 0).reshape(group * rows, cols)

    with jax.named_scope("core_swap"):
        inv = lax.rsqrt(squares / (2 * half) + 1e-05)
        mask = (token_ids[0] != 0).astype(F32)
        note = jnp.concatenate(
            [targets[0].astype(F32), inv[None], mask[None]], axis=0
        )
        note_other = swap(note, "core")
        other = swap(after(mine, copies), "core")
        both = jnp.concatenate([mine, other], axis=0)
        target2 = jnp.concatenate([note[:tokens], note_other[:tokens]], axis=0)
        inv2 = jnp.concatenate([note[tokens], note_other[tokens]])
        mask2 = jnp.concatenate([note[tokens + 1], note_other[tokens + 1]])

    with jax.named_scope("outer_gather"):
        deltas = lax.all_gather(prev_delta[0], WORKER)

    with jax.named_scope("keys"):
        part = jnp.dot(both, matrix, preferred_element_type=F32) * inv2[:, None]
        part = jnp.where(core == side, part - target2, part)
        theirs = swap(part.astype(BF), "tensor")
        scale = (inv2 * mask2)[:, None]
        resid = ((part + theirs.astype(F32)) * scale).astype(BF)

    with jax.named_scope("gradient"):
        term = lax.dot_general(
            both, resid, (((0,), (0,)), ((), ())), preferred_element_type=F32
        ).astype(BF)
        terms = lax.all_to_all(term.reshape(group, rows, cols), GROUP, 0, 0)
        terms, deltas = lax.optimization_barrier((terms, deltas))
        total, partial = sum_terms(terms, 32)
        delta_sum = jnp.sum(deltas.astype(F32), axis=0)

    with jax.named_scope("gradient_home"):
        raw = permute(total, PLANE, lambda yl, x, c, t: (t, x, yl, c))
    with jax.named_scope("norm"):
        partial = lax.all_to_all(partial, PLANE, 0, 0, tiled=True)

    outs = update(
        replicas,
        side.reshape(1),
        fragment_of_tile,
        partial,
        [
            raw,
            adam_first[0],
            adam_second[0],
            weight,
            global_weight,
            outer_momentum,
            delta_sum,
        ],
    )
    return (outs[0][None], outs[1][None], outs[2][None], outs[3], outs[4])


def solution(mesh):
    fine = Mesh(mesh.devices.reshape(*SIZES.values()), tuple(SIZES))
    state = P(WORKER, FSDP, "tensor")
    outer = P(FSDP, "tensor")
    return jax.shard_map(
        local,
        mesh=fine,
        in_specs=(
            P(WORKER, FSDP),
            state,
            state,
            state,
            state,
            state,
            state,
            outer,
            outer,
            P(FSDP, None),
        ),
        out_specs=(state, state, state, outer, outer),
        check_vma=False,
    )
```

```python
import jax
import jax.numpy as jnp
from jax import lax
from jax.experimental import pallas as pl
from jax.experimental.pallas import tpu as pltpu
from jax.sharding import Mesh, PartitionSpec as P

HD = 128
WORKER = "worker"
FSDP = ("ylo", "x", "core")
GROUP = ("x", "ylo")
PLANE = ("ylo", "x", "core", "tensor")
SIZES = {
    "worker": 16,
    "ylo": 2,
    "x": 4,
    "core": 2,
    "tensor": 2,
}
BF = jnp.bfloat16
F32 = jnp.float32
VMEM_LIMIT = 32 * 2**20


def permute(value, axes, move):
    places = [()]
    for axis in axes:
        places = [p + (i,) for p in places for i in range(SIZES[axis])]
    number = {p: n for n, p in enumerate(places)}
    pairs = [(n, number[move(*p)]) for p, n in number.items()]
    return lax.ppermute(value, axes if len(axes) > 1 else axes[0], pairs)


def swap(value, axis):
    return permute(value, (axis,), lambda i: (1 - i,))


def after(value, *others):
    return lax.optimization_barrier((value, *others))[0]


def call(kernel, name, grid, ins, in_specs, outs, out_specs, scratch=(), flops=0):
    moved = sum(a.size * a.dtype.itemsize for a in (*ins, *outs))
    return pl.pallas_call(
        kernel,
        grid=grid,
        in_specs=in_specs,
        out_specs=out_specs,
        out_shape=outs,
        scratch_shapes=scratch,
        name=name,
        compiler_params=pltpu.CompilerParams(vmem_limit_bytes=VMEM_LIMIT),
        cost_estimate=pl.CostEstimate(
            flops=flops, bytes_accessed=moved, transcendentals=0
        ),
    )(*ins)


def sum_kernel(terms, total, squares, so_far):
    step = pl.program_id(0)
    value = jnp.sum(terms[...].astype(F32), axis=0)
    total[...] = value.astype(BF)

    @pl.when(step == 0)
    def _():
        so_far[...] = jnp.zeros_like(so_far)

    so_far[...] += jnp.sum(value * value, axis=0, keepdims=True)

    @pl.when(step == pl.num_programs(0) - 1)
    def _():
        squares[...] = jnp.full(squares.shape, jnp.sum(so_far[...]), F32)


def sum_terms(terms, places):
    group, rows, cols = terms.shape
    part = rows // 4
    return call(
        sum_kernel,
        "sum_terms",
        (rows // part,),
        (terms,),
        [pl.BlockSpec((group, part, cols), lambda k: (0, k, 0))],
        [
            jax.ShapeDtypeStruct((rows, cols), BF),
            jax.ShapeDtypeStruct((places, 128), F32),
        ],
        [
            pl.BlockSpec((part, cols), lambda k: (k, 0)),
            pl.BlockSpec((places, 128), lambda k: (0, 0)),
        ],
        [pltpu.VMEM((1, cols), F32)],
    )


def update_kernel(
    replicas,
    spot,
    fragment,
    squares,
    raw,
    adam_first,
    adam_second,
    weight,
    global_weight,
    outer_momentum,
    delta_sum,
    new_local,
    new_first,
    new_second,
    new_global,
    new_momentum,
):
    step = pl.program_id(0)
    norm = jnp.sqrt(jnp.sum(squares[...], axis=0, keepdims=True)[:, :1])
    clip = jnp.minimum(1.0, 1.0 / (norm + 1e-06))
    heads = raw.shape[1] // HD
    for head in range(heads):
        at = (slice(None), slice(head * HD, (head + 1) * HD))
        clipped = raw[at].astype(F32) * clip
        first = 0.9 * adam_first[at].astype(F32) + 0.1 * clipped
        second = 0.95 * adam_second[at].astype(F32) + 0.05 * clipped * clipped
        old = weight[at].astype(F32)
        stepped = old - 0.0004 * (first / (jnp.sqrt(second) + 1e-08) + 0.1 * old)
        new_first[at] = first.astype(BF)
        new_second[at] = second.astype(BF)
        chosen = fragment[step, spot[0] * heads + head] == 0

        @pl.when(chosen)
        def _():
            outer_grad = delta_sum[at] / replicas
            momentum = 0.9 * outer_momentum[at].astype(F32) + outer_grad
            merged = global_weight[at].astype(F32) - 0.7 * (
                outer_grad + 0.9 * momentum
            )
            merged = merged.astype(BF)
            new_momentum[at] = momentum.astype(BF)
            new_global[at] = merged
            new_local[at] = (0.5 * stepped + 0.5 * merged.astype(F32)).astype(BF)

        @pl.when(jnp.logical_not(chosen))
        def _():
            new_momentum[at] = outer_momentum[at]
            new_global[at] = global_weight[at]
            new_local[at] = stepped.astype(BF)


def update(replicas, spot, fragment, squares, arrays):
    rows, cols = arrays[0].shape
    block = pl.BlockSpec((HD, cols), lambda k: (k, 0))
    smem = pl.BlockSpec(memory_space=pltpu.SMEM)
    return call(
        lambda *refs: update_kernel(replicas, *refs),
        "update",
        (rows // HD,),
        (spot, fragment, squares, *arrays),
        [smem, smem, pl.BlockSpec(squares.shape, lambda k: (0, 0))]
        + [block] * len(arrays),
        [jax.ShapeDtypeStruct((rows, cols), BF)] * 5,
        [block] * 5,
    )


def local(
    token_ids,
    features_in,
    targets,
    local_weight,
    adam_first,
    adam_second,
    prev_delta,
    global_weight,
    outer_momentum,
    fragment_of_tile,
):
    weight = local_weight[0]
    rows, cols = weight.shape
    core = lax.axis_index("core")
    side = lax.axis_index("tensor")
    replicas = lax.axis_size(WORKER)
    group = lax.axis_size("x") * lax.axis_size("ylo")
    mine = features_in[0]
    tokens, half = mine.shape

    with jax.named_scope("weight_move"):
        moved = permute(weight, PLANE, lambda yl, x, c, t: (c, x, t, yl))

    with jax.named_scope("weight_gather"):
        copies = jnp.broadcast_to(moved[None], (group, rows, cols))
        matrix = lax.all_to_all(copies, GROUP, 0, 0).reshape(group * rows, cols)

    with jax.named_scope("core_swap"):
        squares = jnp.sum(jnp.square(mine.astype(F32)), axis=1)
        mask = (token_ids[0] != 0).astype(F32)
        note = jnp.concatenate(
            [targets[0].astype(F32), squares[None], mask[None]], axis=0
        )
        note_other = swap(after(note, copies), "core")
        ready = after(mine, copies)
        other = [swap(ready[at : at + tokens // 2], "core") for at in (0, tokens // 2)]
        both = jnp.concatenate([mine, *other], axis=0)
        target2 = jnp.concatenate([note[:tokens], note_other[:tokens]], axis=0)
        squares2 = jnp.concatenate([note[tokens], note_other[tokens]])
        mask2 = jnp.concatenate([note[tokens + 1], note_other[tokens + 1]])
        squares2 = squares2 + swap(squares2, "tensor")
        inv2 = lax.rsqrt(squares2 / (2 * half) + 1e-05)

    with jax.named_scope("outer_gather"):
        deltas = lax.all_gather(prev_delta[0], WORKER)

    with jax.named_scope("keys"):
        part = jnp.dot(both, matrix, preferred_element_type=F32) * inv2[:, None]
        part = jnp.where(core == side, part - target2, part)
        theirs = swap(part.astype(BF), "tensor")
        scale = (inv2 * mask2)[:, None]
        resid = ((part + theirs.astype(F32)) * scale).astype(BF)

    with jax.named_scope("gradient"):
        term = lax.dot_general(
            both, resid, (((0,), (0,)), ((), ())), preferred_element_type=F32
        ).astype(BF)
        terms = lax.all_to_all(term.reshape(group, rows, cols), GROUP, 0, 0)
        terms, deltas = lax.optimization_barrier((terms, deltas))
        total, partial = sum_terms(terms, 32)
        delta_sum = jnp.sum(deltas.astype(F32), axis=0)

    with jax.named_scope("gradient_home"):
        raw = permute(total, PLANE, lambda yl, x, c, t: (t, x, yl, c))
    with jax.named_scope("norm"):
        partial = lax.all_to_all(partial, PLANE, 0, 0, tiled=True)

    outs = update(
        replicas,
        side.reshape(1),
        fragment_of_tile,
        partial,
        [
            raw,
            adam_first[0],
            adam_second[0],
            weight,
            global_weight,
            outer_momentum,
            delta_sum,
        ],
    )
    return (outs[0][None], outs[1][None], outs[2][None], outs[3], outs[4])


def solution(mesh):
    fine = Mesh(mesh.devices.reshape(*SIZES.values()), tuple(SIZES))
    state = P(WORKER, FSDP, "tensor")
    outer = P(FSDP, "tensor")
    return jax.shard_map(
        local,
        mesh=fine,
        in_specs=(
            P(WORKER, FSDP),
            state,
            state,
            state,
            state,
            state,
            state,
            outer,
            outer,
            P(FSDP, None),
        ),
        out_specs=(state, state, state, outer, outer),
        check_vma=False,
    )
```

```python
import itertools

import jax
import jax.numpy as jnp
from jax import lax
from jax.experimental import pallas as pl
from jax.experimental.pallas import tpu as pltpu
from jax.sharding import Mesh, PartitionSpec as P

HD = 128
WORKER = "worker"
FSDP = ("ylo", "x", "core")
GROUP = ("x", "ylo")
PLANE = ("ylo", "x", "core", "tensor")
SIZES = {
    "worker": 16,
    "ylo": 2,
    "x": 4,
    "core": 2,
    "tensor": 2,
}
BF = jnp.bfloat16
F32 = jnp.float32
VMEM_LIMIT = 8 * 2**20


def permute(value, axes, move):
    places = [()]
    for axis in axes:
        places = [p + (i,) for p in places for i in range(SIZES[axis])]
    number = {p: n for n, p in enumerate(places)}
    pairs = [(n, number[move(*p)]) for p, n in number.items()]
    return lax.ppermute(value, axes if len(axes) > 1 else axes[0], pairs)


def swap(value, axis):
    return permute(value, (axis,), lambda i: (1 - i,))


def after(value, *others):
    return lax.optimization_barrier((value, *others))[0]


def call(kernel, name, grid, ins, in_specs, outs, out_specs, scratch=(), flops=0, vmem=VMEM_LIMIT):
    moved = sum(a.size * a.dtype.itemsize for a in (*ins, *outs))
    return pl.pallas_call(
        kernel,
        grid=grid,
        in_specs=in_specs,
        out_specs=out_specs,
        out_shape=outs,
        scratch_shapes=scratch,
        name=name,
        compiler_params=pltpu.CompilerParams(vmem_limit_bytes=vmem),
        cost_estimate=pl.CostEstimate(
            flops=flops, bytes_accessed=moved, transcendentals=0
        ),
    )(*ins)


def keys_kernel(both, matrix, scale, target, part, low, total):
    step = pl.program_id(0)
    value = jnp.dot(both[...], matrix[...], preferred_element_type=F32)

    @pl.when(step == 0)
    def _():
        total[...] = value

    @pl.when(step == 1)
    def _():
        keys = (total[...] + value) * scale[...] - target[...]
        part[...] = keys
        low[...] = keys.astype(BF)


def partial_keys(both, matrix, scale, target):
    tokens, half = both.shape
    cols = matrix.shape[1]
    depth = half // 2
    outs = [
        jax.ShapeDtypeStruct((tokens, cols), F32),
        jax.ShapeDtypeStruct((tokens, cols), BF),
    ]
    full = pl.BlockSpec((tokens, cols), lambda k: (0, 0))
    return call(
        keys_kernel,
        "partial_keys",
        (2,),
        (both, matrix, scale, target),
        [
            pl.BlockSpec((tokens, depth), lambda k: (0, k)),
            pl.BlockSpec((depth, cols), lambda k: (k, 0)),
            full,
            full,
        ],
        outs,
        [full, full],
        [pltpu.VMEM((tokens, cols), F32)],
        2 * tokens * half * cols,
        48 * 2**20,
    )


def sum_kernel(terms, total, squares, so_far):
    step = pl.program_id(0)
    value = jnp.sum(terms[...].astype(F32), axis=0)
    total[...] = value.astype(BF)

    @pl.when(step == 0)
    def _():
        so_far[...] = jnp.zeros_like(so_far)

    so_far[...] += jnp.sum(value * value, axis=0, keepdims=True)

    @pl.when(step == pl.num_programs(0) - 1)
    def _():
        squares[...] = jnp.full(squares.shape, jnp.sum(so_far[...]), F32)


def sum_terms(terms, places):
    group, rows, cols = terms.shape
    part = rows // 2
    return call(
        sum_kernel,
        "sum_terms",
        (rows // part,),
        (terms,),
        [pl.BlockSpec((group, part, cols), lambda k: (0, k, 0))],
        [
            jax.ShapeDtypeStruct((rows, cols), BF),
            jax.ShapeDtypeStruct((places, 128), F32),
        ],
        [
            pl.BlockSpec((part, cols), lambda k: (k, 0)),
            pl.BlockSpec((places, 128), lambda k: (0, 0)),
        ],
        [pltpu.VMEM((1, cols), F32)],
    )


def update_kernel(
    replicas,
    spot,
    fragment,
    squares,
    raw,
    adam_first,
    adam_second,
    weight,
    global_weight,
    outer_momentum,
    delta_sum,
    new_local,
    new_first,
    new_second,
    new_global,
    new_momentum,
):
    step = pl.program_id(0)
    norm = jnp.sqrt(jnp.sum(squares[...], axis=0, keepdims=True)[:, :1])
    clip = jnp.minimum(1.0, 1.0 / (norm + 1e-06))
    heads = raw.shape[1] // HD
    tiles = raw.shape[0] // HD
    for tile, head in itertools.product(range(tiles), range(heads)):
        at = (slice(tile * HD, (tile + 1) * HD), slice(head * HD, (head + 1) * HD))
        clipped = raw[at].astype(F32) * clip
        first = 0.9 * adam_first[at].astype(F32) + 0.1 * clipped
        second = 0.95 * adam_second[at].astype(F32) + 0.05 * clipped * clipped
        old = weight[at].astype(F32)
        stepped = old - 0.0004 * (first / (jnp.sqrt(second) + 1e-08) + 0.1 * old)
        new_first[at] = first.astype(BF)
        new_second[at] = second.astype(BF)
        chosen = fragment[step * tiles + tile, spot[0] * heads + head] == 0

        @pl.when(chosen)
        def _():
            outer_grad = delta_sum[at] / replicas
            momentum = 0.9 * outer_momentum[at].astype(F32) + outer_grad
            merged = global_weight[at].astype(F32) - 0.7 * (
                outer_grad + 0.9 * momentum
            )
            merged = merged.astype(BF)
            new_momentum[at] = momentum.astype(BF)
            new_global[at] = merged
            new_local[at] = (0.5 * stepped + 0.5 * merged.astype(F32)).astype(BF)

        @pl.when(jnp.logical_not(chosen))
        def _():
            new_momentum[at] = outer_momentum[at]
            new_global[at] = global_weight[at]
            new_local[at] = stepped.astype(BF)


def update(replicas, spot, fragment, squares, arrays):
    rows, cols = arrays[0].shape
    block = pl.BlockSpec((rows // 2, cols), lambda k: (k, 0))
    smem = pl.BlockSpec(memory_space=pltpu.SMEM)
    return call(
        lambda *refs: update_kernel(replicas, *refs),
        "update",
        (2,),
        (spot, fragment, squares, *arrays),
        [smem, smem, pl.BlockSpec(squares.shape, lambda k: (0, 0))]
        + [block] * len(arrays),
        [jax.ShapeDtypeStruct((rows, cols), BF)] * 5,
        [block] * 5,
    )


def local(
    token_ids,
    features_in,
    targets,
    local_weight,
    adam_first,
    adam_second,
    prev_delta,
    global_weight,
    outer_momentum,
    fragment_of_tile,
):
    weight = local_weight[0]
    rows, cols = weight.shape
    core = lax.axis_index("core")
    side = lax.axis_index("tensor")
    replicas = lax.axis_size(WORKER)
    group = lax.axis_size("x") * lax.axis_size("ylo")
    mine = features_in[0]
    tokens, half = mine.shape

    with jax.named_scope("weight_move"):
        moved = permute(weight, PLANE, lambda yl, x, c, t: (c, x, t, yl))

    with jax.named_scope("weight_gather"):
        copies = jnp.broadcast_to(moved[None], (group, rows, cols))
        matrix = lax.all_to_all(copies, GROUP, 0, 0).reshape(group * rows, cols)

    with jax.named_scope("core_swap"):
        squares = jnp.sum(jnp.square(mine.astype(F32)), axis=1)
        mask = (token_ids[0] != 0).astype(F32)
        note = jnp.concatenate(
            [targets[0].astype(F32), squares[None], mask[None]], axis=0
        )
        note_other = swap(after(note, copies), "core")
        ready = after(mine, copies)
        other = [swap(ready[at : at + tokens // 2], "core") for at in (0, tokens // 2)]
        both = jnp.concatenate([mine, *other], axis=0)
        target2 = jnp.concatenate([note[:tokens], note_other[:tokens]], axis=0)
        squares2 = jnp.concatenate([note[tokens], note_other[tokens]])
        mask2 = jnp.concatenate([note[tokens + 1], note_other[tokens + 1]])
        squares2 = squares2 + swap(squares2, "tensor")
        inv2 = lax.rsqrt(squares2 / (2 * half) + 1e-05)

    with jax.named_scope("outer_gather"):
        deltas = lax.all_gather(prev_delta[0], WORKER)

    with jax.named_scope("keys"):
        shape = (2 * tokens, cols)
        spread = jnp.broadcast_to(inv2[:, None], shape)
        shift = jnp.where(core == side, target2, 0.0)
        both, spread, shift, matrix = lax.optimization_barrier(
            (both, spread, shift, matrix)
        )
        part, low = partial_keys(both, matrix, spread, shift)
        theirs = swap(low, "tensor")
        scale = (inv2 * mask2)[:, None]
        resid = ((part + theirs.astype(F32)) * scale).astype(BF)

    with jax.named_scope("gradient"):
        term = lax.dot_general(
            both, resid, (((0,), (0,)), ((), ())), preferred_element_type=F32
        ).astype(BF)
        terms = lax.all_to_all(term.reshape(group, rows, cols), GROUP, 0, 0)
        terms, deltas = lax.optimization_barrier((terms, deltas))
        total, partial = sum_terms(terms, 32)
        delta_sum = jnp.sum(deltas.astype(F32), axis=0)

    with jax.named_scope("gradient_home"):
        raw = permute(total, PLANE, lambda yl, x, c, t: (t, x, yl, c))
    with jax.named_scope("norm"):
        partial = lax.all_to_all(partial, PLANE, 0, 0, tiled=True)

    outs = update(
        replicas,
        side.reshape(1),
        fragment_of_tile,
        partial,
        [
            raw,
            adam_first[0],
            adam_second[0],
            weight,
            global_weight,
            outer_momentum,
            delta_sum,
        ],
    )
    return (outs[0][None], outs[1][None], outs[2][None], outs[3], outs[4])


def solution(mesh):
    fine = Mesh(mesh.devices.reshape(*SIZES.values()), tuple(SIZES))
    state = P(WORKER, FSDP, "tensor")
    outer = P(FSDP, "tensor")
    return jax.shard_map(
        local,
        mesh=fine,
        in_specs=(
            P(WORKER, FSDP),
            state,
            state,
            state,
            state,
            state,
            state,
            outer,
            outer,
            P(FSDP, None),
        ),
        out_specs=(state, state, state, outer, outer),
        check_vma=False,
    )
```

```python
import itertools

import jax
import jax.numpy as jnp
from jax import lax
from jax.experimental import pallas as pl
from jax.experimental.pallas import tpu as pltpu
from jax.sharding import Mesh, PartitionSpec as P

HD = 128
WORKER = "worker"
FSDP = ("ylo", "x", "core")
GROUP = ("x", "ylo")
PLANE = ("ylo", "x", "core", "tensor")
SIZES = {
    "worker": 16,
    "ylo": 2,
    "x": 4,
    "core": 2,
    "tensor": 2,
}
BF = jnp.bfloat16
F32 = jnp.float32
VMEM_LIMIT = 8 * 2**20


def permute(value, axes, move):
    places = [()]
    for axis in axes:
        places = [p + (i,) for p in places for i in range(SIZES[axis])]
    number = {p: n for n, p in enumerate(places)}
    pairs = [(n, number[move(*p)]) for p, n in number.items()]
    return lax.ppermute(value, axes if len(axes) > 1 else axes[0], pairs)


def swap(value, axis):
    return permute(value, (axis,), lambda i: (1 - i,))


def after(value, *others):
    return lax.optimization_barrier((value, *others))[0]


def call(kernel, name, grid, ins, in_specs, outs, out_specs, scratch=(), flops=0, vmem=VMEM_LIMIT):
    moved = sum(a.size * a.dtype.itemsize for a in (*ins, *outs))
    return pl.pallas_call(
        kernel,
        grid=grid,
        in_specs=in_specs,
        out_specs=out_specs,
        out_shape=outs,
        scratch_shapes=scratch,
        name=name,
        compiler_params=pltpu.CompilerParams(vmem_limit_bytes=vmem),
        cost_estimate=pl.CostEstimate(
            flops=flops, bytes_accessed=moved, transcendentals=0
        ),
    )(*ins)


def keys_kernel(both, matrix, scale, target, part, low, total):
    step = pl.program_id(0)
    value = jnp.dot(both[...], matrix[...], preferred_element_type=F32)

    @pl.when(step == 0)
    def _():
        total[...] = value

    @pl.when(step == 1)
    def _():
        inv = scale[...]
        keys = jnp.where(inv == 0, 0.0, (total[...] + value) * inv) - target[...]
        part[...] = keys
        low[...] = keys.astype(BF)


def partial_keys(both, matrix, scale, target):
    tokens, half = both.shape
    cols = matrix.shape[1]
    depth = half // 2
    outs = [
        jax.ShapeDtypeStruct((tokens, cols), F32),
        jax.ShapeDtypeStruct((tokens, cols), BF),
    ]
    full = pl.BlockSpec((tokens, cols), lambda k: (0, 0))
    return call(
        keys_kernel,
        "partial_keys",
        (2,),
        (both, matrix, scale, target),
        [
            pl.BlockSpec((tokens, depth), lambda k: (0, k)),
            pl.BlockSpec((depth, cols), lambda k: (k, 0)),
            full,
            full,
        ],
        outs,
        [full, full],
        [pltpu.VMEM((tokens, cols), F32)],
        2 * tokens * half * cols,
        48 * 2**20,
    )


def sum_kernel(terms, total, squares, so_far):
    step = pl.program_id(0)
    value = jnp.sum(terms[...].astype(F32), axis=0)
    total[...] = value.astype(BF)

    @pl.when(step == 0)
    def _():
        so_far[...] = jnp.zeros_like(so_far)

    so_far[...] += jnp.sum(value * value, axis=0, keepdims=True)

    @pl.when(step == pl.num_programs(0) - 1)
    def _():
        squares[...] = jnp.full(squares.shape, jnp.sum(so_far[...]), F32)


def sum_terms(terms, places):
    group, rows, cols = terms.shape
    part = rows // 2
    return call(
        sum_kernel,
        "sum_terms",
        (rows // part,),
        (terms,),
        [pl.BlockSpec((group, part, cols), lambda k: (0, k, 0))],
        [
            jax.ShapeDtypeStruct((rows, cols), BF),
            jax.ShapeDtypeStruct((places, 128), F32),
        ],
        [
            pl.BlockSpec((part, cols), lambda k: (k, 0)),
            pl.BlockSpec((places, 128), lambda k: (0, 0)),
        ],
        [pltpu.VMEM((1, cols), F32)],
    )


def update_kernel(
    replicas,
    spot,
    fragment,
    squares,
    raw,
    adam_first,
    adam_second,
    weight,
    global_weight,
    outer_momentum,
    delta_sum,
    new_local,
    new_first,
    new_second,
    new_global,
    new_momentum,
):
    step = pl.program_id(0)
    norm = jnp.sqrt(jnp.sum(squares[...], axis=0, keepdims=True)[:, :1])
    clip = jnp.minimum(1.0, 1.0 / (norm + 1e-06))
    heads = raw.shape[1] // HD
    tiles = raw.shape[0] // HD
    for tile, head in itertools.product(range(tiles), range(heads)):
        at = (slice(tile * HD, (tile + 1) * HD), slice(head * HD, (head + 1) * HD))
        clipped = raw[at].astype(F32) * clip
        first = 0.9 * adam_first[at].astype(F32) + 0.1 * clipped
        second = 0.95 * adam_second[at].astype(F32) + 0.05 * clipped * clipped
        old = weight[at].astype(F32)
        stepped = old - 0.0004 * (first / (jnp.sqrt(second) + 1e-08) + 0.1 * old)
        new_first[at] = first.astype(BF)
        new_second[at] = second.astype(BF)
        chosen = fragment[step * tiles + tile, spot[0] * heads + head] == 0

        @pl.when(chosen)
        def _():
            outer_grad = delta_sum[at] / replicas
            momentum = 0.9 * outer_momentum[at].astype(F32) + outer_grad
            merged = global_weight[at].astype(F32) - 0.7 * (
                outer_grad + 0.9 * momentum
            )
            merged = merged.astype(BF)
            new_momentum[at] = momentum.astype(BF)
            new_global[at] = merged
            new_local[at] = (0.5 * stepped + 0.5 * merged.astype(F32)).astype(BF)

        @pl.when(jnp.logical_not(chosen))
        def _():
            new_momentum[at] = outer_momentum[at]
            new_global[at] = global_weight[at]
            new_local[at] = stepped.astype(BF)


def update(replicas, spot, fragment, squares, arrays):
    rows, cols = arrays[0].shape
    block = pl.BlockSpec((rows // 2, cols), lambda k: (k, 0))
    smem = pl.BlockSpec(memory_space=pltpu.SMEM)
    return call(
        lambda *refs: update_kernel(replicas, *refs),
        "update",
        (2,),
        (spot, fragment, squares, *arrays),
        [smem, smem, pl.BlockSpec(squares.shape, lambda k: (0, 0))]
        + [block] * len(arrays),
        [jax.ShapeDtypeStruct((rows, cols), BF)] * 5,
        [block] * 5,
    )


def local(
    token_ids,
    features_in,
    targets,
    local_weight,
    adam_first,
    adam_second,
    prev_delta,
    global_weight,
    outer_momentum,
    fragment_of_tile,
):
    weight = local_weight[0]
    rows, cols = weight.shape
    core = lax.axis_index("core")
    side = lax.axis_index("tensor")
    replicas = lax.axis_size(WORKER)
    group = lax.axis_size("x") * lax.axis_size("ylo")
    mine = features_in[0]
    tokens, half = mine.shape

    with jax.named_scope("weight_move"):
        moved = permute(weight, PLANE, lambda yl, x, c, t: (c, x, t, yl))

    with jax.named_scope("weight_gather"):
        copies = jnp.broadcast_to(moved[None], (group, rows, cols))
        matrix = lax.all_to_all(copies, GROUP, 0, 0).reshape(group * rows, cols)

    with jax.named_scope("core_swap"):
        squares = jnp.sum(jnp.square(mine.astype(F32)), axis=1)
        mask = (token_ids[0] != 0).astype(F32)
        note = jnp.concatenate(
            [targets[0].astype(F32), squares[None], mask[None]], axis=0
        )
        note_other = swap(after(note, copies), "core")
        ready = after(mine, copies)
        other = [swap(ready[at : at + tokens // 2], "core") for at in (0, tokens // 2)]
        both = jnp.concatenate([mine, *other], axis=0)
        target2 = jnp.concatenate([note[:tokens], note_other[:tokens]], axis=0)
        squares2 = jnp.concatenate([note[tokens], note_other[tokens]])
        mask2 = jnp.concatenate([note[tokens + 1], note_other[tokens + 1]])
        squares2 = squares2 + swap(squares2, "tensor")
        inv2 = lax.rsqrt(squares2 / (2 * half) + 1e-05)

    with jax.named_scope("outer_gather"):
        deltas = lax.all_gather(prev_delta[0], WORKER)

    with jax.named_scope("keys"):
        shape = (2 * tokens, cols)
        spread = jnp.broadcast_to(inv2[:, None], shape)
        shift = jnp.where(core == side, target2, 0.0)
        both, spread, shift, matrix = lax.optimization_barrier(
            (both, spread, shift, matrix)
        )
        part, low = partial_keys(both, matrix, spread, shift)
        theirs = swap(low, "tensor")
        scale = (inv2 * mask2)[:, None]
        resid = ((part + theirs.astype(F32)) * scale).astype(BF)

    with jax.named_scope("gradient"):
        term = lax.dot_general(
            both, resid, (((0,), (0,)), ((), ())), preferred_element_type=F32
        ).astype(BF)
        terms = lax.all_to_all(term.reshape(group, rows, cols), GROUP, 0, 0)
        terms, deltas = lax.optimization_barrier((terms, deltas))
        total, partial = sum_terms(terms, 32)
        delta_sum = jnp.sum(deltas.astype(F32), axis=0)

    with jax.named_scope("gradient_home"):
        raw = permute(total, PLANE, lambda yl, x, c, t: (t, x, yl, c))
    with jax.named_scope("norm"):
        partial = lax.all_to_all(partial, PLANE, 0, 0, tiled=True)

    outs = update(
        replicas,
        side.reshape(1),
        fragment_of_tile,
        partial,
        [
            raw,
            adam_first[0],
            adam_second[0],
            weight,
            global_weight,
            outer_momentum,
            delta_sum,
        ],
    )
    return (outs[0][None], outs[1][None], outs[2][None], outs[3], outs[4])


def solution(mesh):
    fine = Mesh(mesh.devices.reshape(*SIZES.values()), tuple(SIZES))
    state = P(WORKER, FSDP, "tensor")
    outer = P(FSDP, "tensor")
    return jax.shard_map(
        local,
        mesh=fine,
        in_specs=(
            P(WORKER, FSDP),
            state,
            state,
            state,
            state,
            state,
            state,
            outer,
            outer,
            P(FSDP, None),
        ),
        out_specs=(state, state, state, outer, outer),
        check_vma=False,
    )
```

```python
import itertools

import jax
import jax.numpy as jnp
from jax import lax
from jax.experimental import pallas as pl
from jax.experimental.pallas import tpu as pltpu
from jax.sharding import Mesh, PartitionSpec as P

HD = 128
WORKER = "worker"
FSDP = ("ylo", "x", "core")
GROUP = ("x", "ylo")
PLANE = ("ylo", "x", "core", "tensor")
SIZES = {
    "worker": 16,
    "ylo": 2,
    "x": 4,
    "core": 2,
    "tensor": 2,
}
BF = jnp.bfloat16
F32 = jnp.float32
VMEM_LIMIT = 8 * 2**20


def permute(value, axes, move):
    places = [()]
    for axis in axes:
        places = [p + (i,) for p in places for i in range(SIZES[axis])]
    number = {p: n for n, p in enumerate(places)}
    pairs = [(n, number[move(*p)]) for p, n in number.items()]
    return lax.ppermute(value, axes if len(axes) > 1 else axes[0], pairs)


def swap(value, axis):
    return permute(value, (axis,), lambda i: (1 - i,))


def after(value, *others):
    return lax.optimization_barrier((value, *others))[0]


def call(kernel, name, grid, ins, in_specs, outs, out_specs, scratch=(), flops=0, vmem=VMEM_LIMIT):
    moved = sum(a.size * a.dtype.itemsize for a in (*ins, *outs))
    return pl.pallas_call(
        kernel,
        grid=grid,
        in_specs=in_specs,
        out_specs=out_specs,
        out_shape=outs,
        scratch_shapes=scratch,
        name=name,
        compiler_params=pltpu.CompilerParams(vmem_limit_bytes=vmem),
        cost_estimate=pl.CostEstimate(
            flops=flops, bytes_accessed=moved, transcendentals=0
        ),
    )(*ins)


def keys_kernel(both, matrix, scale, target, low, total):
    step = pl.program_id(0)
    value = jnp.dot(both[...], matrix[...], preferred_element_type=F32)

    @pl.when(step == 0)
    def _():
        total[...] = value

    @pl.when(step == 1)
    def _():
        inv = scale[...]
        keys = jnp.where(inv == 0, 0.0, (total[...] + value) * inv)
        keys -= target[...].astype(F32)
        low[...] = keys.astype(BF)


def partial_keys(both, matrix, scale, target):
    tokens, half = both.shape
    cols = matrix.shape[1]
    depth = half // 2
    outs = [
        jax.ShapeDtypeStruct((tokens, cols), BF),
    ]
    full = pl.BlockSpec((tokens, cols), lambda k: (0, 0))
    return call(
        keys_kernel,
        "partial_keys",
        (2,),
        (both, matrix, scale, target),
        [
            pl.BlockSpec((tokens, depth), lambda k: (0, k)),
            pl.BlockSpec((depth, cols), lambda k: (k, 0)),
            full,
            full,
        ],
        outs,
        [full],
        [pltpu.VMEM((tokens, cols), F32)],
        2 * tokens * half * cols,
        48 * 2**20,
    )


def sum_kernel(terms, total, squares, so_far):
    step = pl.program_id(0)
    value = jnp.sum(terms[...].astype(F32), axis=0)
    total[...] = value.astype(BF)

    @pl.when(step == 0)
    def _():
        so_far[...] = jnp.zeros_like(so_far)

    so_far[...] += jnp.sum(value * value, axis=0, keepdims=True)

    @pl.when(step == pl.num_programs(0) - 1)
    def _():
        squares[...] = jnp.full(squares.shape, jnp.sum(so_far[...]), F32)


def sum_terms(terms, places):
    group, rows, cols = terms.shape
    part = rows // 2
    return call(
        sum_kernel,
        "sum_terms",
        (rows // part,),
        (terms,),
        [pl.BlockSpec((group, part, cols), lambda k: (0, k, 0))],
        [
            jax.ShapeDtypeStruct((rows, cols), BF),
            jax.ShapeDtypeStruct((places, 128), F32),
        ],
        [
            pl.BlockSpec((part, cols), lambda k: (k, 0)),
            pl.BlockSpec((places, 128), lambda k: (0, 0)),
        ],
        [pltpu.VMEM((1, cols), F32)],
    )


def update_kernel(
    replicas,
    spot,
    fragment,
    squares,
    raw,
    adam_first,
    adam_second,
    weight,
    global_weight,
    outer_momentum,
    delta_sum,
    new_local,
    new_first,
    new_second,
    new_global,
    new_momentum,
):
    step = pl.program_id(0)
    norm = jnp.sqrt(jnp.sum(squares[...], axis=0, keepdims=True)[:, :1])
    clip = jnp.minimum(1.0, 1.0 / (norm + 1e-06))
    heads = raw.shape[1] // HD
    tiles = raw.shape[0] // HD
    for tile, head in itertools.product(range(tiles), range(heads)):
        at = (slice(tile * HD, (tile + 1) * HD), slice(head * HD, (head + 1) * HD))
        clipped = raw[at].astype(F32) * clip
        first = 0.9 * adam_first[at].astype(F32) + 0.1 * clipped
        second = 0.95 * adam_second[at].astype(F32) + 0.05 * clipped * clipped
        old = weight[at].astype(F32)
        stepped = old - 0.0004 * (first / (jnp.sqrt(second) + 1e-08) + 0.1 * old)
        new_first[at] = first.astype(BF)
        new_second[at] = second.astype(BF)
        chosen = fragment[step * tiles + tile, spot[0] * heads + head] == 0

        @pl.when(chosen)
        def _():
            outer_grad = delta_sum[at] / replicas
            momentum = 0.9 * outer_momentum[at].astype(F32) + outer_grad
            merged = global_weight[at].astype(F32) - 0.7 * (
                outer_grad + 0.9 * momentum
            )
            merged = merged.astype(BF)
            new_momentum[at] = momentum.astype(BF)
            new_global[at] = merged
            new_local[at] = (0.5 * stepped + 0.5 * merged.astype(F32)).astype(BF)

        @pl.when(jnp.logical_not(chosen))
        def _():
            new_momentum[at] = outer_momentum[at]
            new_global[at] = global_weight[at]
            new_local[at] = stepped.astype(BF)


def update(replicas, spot, fragment, squares, arrays):
    rows, cols = arrays[0].shape
    block = pl.BlockSpec((rows // 2, cols), lambda k: (k, 0))
    smem = pl.BlockSpec(memory_space=pltpu.SMEM)
    return call(
        lambda *refs: update_kernel(replicas, *refs),
        "update",
        (2,),
        (spot, fragment, squares, *arrays),
        [smem, smem, pl.BlockSpec(squares.shape, lambda k: (0, 0))]
        + [block] * len(arrays),
        [jax.ShapeDtypeStruct((rows, cols), BF)] * 5,
        [block] * 5,
    )


def local(
    token_ids,
    features_in,
    targets,
    local_weight,
    adam_first,
    adam_second,
    prev_delta,
    global_weight,
    outer_momentum,
    fragment_of_tile,
):
    weight = local_weight[0]
    rows, cols = weight.shape
    core = lax.axis_index("core")
    side = lax.axis_index("tensor")
    replicas = lax.axis_size(WORKER)
    group = lax.axis_size("x") * lax.axis_size("ylo")
    mine = features_in[0]
    tokens, half = mine.shape

    with jax.named_scope("weight_move"):
        moved = permute(weight, PLANE, lambda yl, x, c, t: (c, x, t, yl))

    with jax.named_scope("weight_gather"):
        copies = jnp.broadcast_to(moved[None], (group, rows, cols))
        matrix = lax.all_to_all(copies, GROUP, 0, 0).reshape(group * rows, cols)

    with jax.named_scope("core_swap"):
        squares = jnp.sum(jnp.square(mine.astype(F32)), axis=1)
        mask = (token_ids[0] != 0).astype(F32)
        note = jnp.concatenate(
            [targets[0].astype(F32), squares[None], mask[None]], axis=0
        )
        note_other = swap(after(note, copies), "core")
        ready = after(mine, copies)
        other = [swap(ready[at : at + tokens // 2], "core") for at in (0, tokens // 2)]
        both = jnp.concatenate([mine, *other], axis=0)
        target2 = jnp.concatenate([note[:tokens], note_other[:tokens]], axis=0)
        squares2 = jnp.concatenate([note[tokens], note_other[tokens]])
        mask2 = jnp.concatenate([note[tokens + 1], note_other[tokens + 1]])
        squares2 = squares2 + swap(squares2, "tensor")
        inv2 = lax.rsqrt(squares2 / (2 * half) + 1e-05)

    with jax.named_scope("outer_gather"):
        deltas = lax.all_gather(prev_delta[0], WORKER)

    with jax.named_scope("keys"):
        shape = (2 * tokens, cols)
        spread = jnp.broadcast_to(inv2[:, None], shape)
        shift = jnp.where(core == side, target2, 0.0).astype(BF)
        both, spread, shift, matrix = lax.optimization_barrier(
            (both, spread, shift, matrix)
        )
        (part,) = partial_keys(both, matrix, spread, shift)
        theirs = swap(part, "tensor")
        scale = (inv2 * mask2)[:, None]
        resid = ((part.astype(F32) + theirs.astype(F32)) * scale).astype(BF)

    with jax.named_scope("gradient"):
        term = lax.dot_general(
            both, resid, (((0,), (0,)), ((), ())), preferred_element_type=F32
        ).astype(BF)
        terms = lax.all_to_all(term.reshape(group, rows, cols), GROUP, 0, 0)
        terms, deltas = lax.optimization_barrier((terms, deltas))
        total, partial = sum_terms(terms, 32)
        delta_sum = jnp.sum(deltas.astype(F32), axis=0)

    with jax.named_scope("gradient_home"):
        raw = permute(total, PLANE, lambda yl, x, c, t: (t, x, yl, c))
    with jax.named_scope("norm"):
        partial = lax.all_to_all(partial, PLANE, 0, 0, tiled=True)

    outs = update(
        replicas,
        side.reshape(1),
        fragment_of_tile,
        partial,
        [
            raw,
            adam_first[0],
            adam_second[0],
            weight,
            global_weight,
            outer_momentum,
            delta_sum,
        ],
    )
    return (outs[0][None], outs[1][None], outs[2][None], outs[3], outs[4])


def solution(mesh):
    fine = Mesh(mesh.devices.reshape(*SIZES.values()), tuple(SIZES))
    state = P(WORKER, FSDP, "tensor")
    outer = P(FSDP, "tensor")
    return jax.shard_map(
        local,
        mesh=fine,
        in_specs=(
            P(WORKER, FSDP),
            state,
            state,
            state,
            state,
            state,
            state,
            outer,
            outer,
            P(FSDP, None),
        ),
        out_specs=(state, state, state, outer, outer),
        check_vma=False,
    )
```
